256 devices in a mesh: row: 8 (over y_hi, x), col: 32 (over y_lo, z, core).
Axes of the slice: x: 4, y: 4 (y_hi: 2, y_lo: 2; y = y_hi * 2 + y_lo), z: 8, core: 2. Of those that a mesh axis runs over, the one named last changes fastest.
Arguments:
- intensity: float32 [16, 2048, 2048], P(None, 'row', 'col'), may hold values from -6 to 6
- punch_radius: int32 [2, 129, 129], replicated, may hold values from 0 to 12
Outputs:
- out_re: float32 [16, 2048, 2048], P(None, ('row', 'col'))
- out_im: float32 [16, 2048, 2048], P(None, ('row', 'col'))
The draws below stay inside these ranges and needn't reach their ends.
Inputs may be any that keep to these rules, and one draw needn't show every extreme that they name: `punch_radius`: squared radius in voxels; 0 leaves a node unpunched.
All inputs are finite; a program needn't handle non-finite values.
Results may differ from the reference program's by a relative error of at most 0.0029.
Values may be sent and summed in bfloat16 or wider, within the bound.
No kernel may reach another device: no remote copies, remote signals or barrier semaphores. Data moves between devices by JAX's collectives and lax.ppermute only.
A program may use at most 128 MiB of HBM per device.

```python
import math
import jax
import jax.numpy as jnp
from jax import lax

N = 2048
SP = 16
L = 16
NODES = 128
LNODES = 2


def plant(array, own_key, smallest, largest):
    longest = array.shape.index(max(array.shape))
    spots = []
    for shift in (0, 1):
        where = [jax.random.randint(jax.random.fold_in(own_key, axis), (), 0, length) for axis, length in enumerate(array.shape)]
        where[longest] = (where[longest] + shift) % array.shape[longest]
        spots.append(tuple(where))
    return array.at[spots[0]].set(smallest).at[spots[1]].set(largest)


def block_scale(key, shape, cuts, least, high):
    gain = 1.0
    for position, parts in cuts:
        heights = jax.random.uniform(jax.random.fold_in(jax.random.fold_in(key, 6), position), (parts,), jnp.float32, least / len(cuts), high / len(cuts))
        gain = gain * jnp.repeat(jnp.exp(heights), shape[position] // parts).reshape((-1,) + (1,) * (len(shape) - 1 - position))
    return gain


def noise(key, extent, scale, reach, pieces=(), held_as=jnp.bfloat16):
    gain = block_scale(key, extent, pieces, -0.22, 0.18) if pieces else 1.0
    array = jax.random.normal(key, extent, jnp.float32) * scale * gain
    return jnp.minimum(jnp.maximum(array, -reach), reach).astype(held_as)


def setup_inputs(seed: int = 0) -> dict:
    splits = jax.random.split(jax.random.key(seed), 3)
    return {
        "intensity": noise(splits[0], (L, N, N), 1.0, 6.0, ((1, 8), (2, 32)), jnp.float32),
        "punch_radius": plant(jax.random.randint(splits[1], (LNODES, NODES + 1, NODES + 1), 0, 13), jax.random.fold_in(splits[1], 1), 0, 12).astype(jnp.int32),
    }


def circle(count, period, width):
    first_ids = jnp.arange(count, dtype=jnp.int32)
    second_ids = jnp.arange(width, dtype=jnp.int32)
    phases = (first_ids[:, None] * second_ids[None, :]) % period
    angles = phases.astype(jnp.float32) * (2.0 * math.pi / period)
    return jnp.cos(angles), jnp.sin(angles)


def mixed(form, left, right):
    return jnp.einsum(form, left, right, precision=lax.Precision.HIGHEST)


def spectral(real_in, imag_in):
    length = real_in.shape[-1]
    first = 32
    second = length // first
    shape_lead = real_in.shape[:-1]
    cos_first, sin_first = circle(first, first, first)
    cos_twist, sin_twist = circle(first, length, second)
    cos_second, sin_second = circle(second, second, second)
    grid_re = real_in.reshape(shape_lead + (first, second))
    section_re = mixed('...ab,ac->...cb', grid_re, cos_first)
    section_im = mixed('...ab,ac->...cb', grid_re, sin_first)
    if imag_in is not None:
        grid_im = imag_in.reshape(shape_lead + (first, second))
        section_re = section_re - mixed('...ab,ac->...cb', grid_im, sin_first)
        section_im = section_im + mixed('...ab,ac->...cb', grid_im, cos_first)
    twist_re = section_re * cos_twist - section_im * sin_twist
    twist_im = section_re * sin_twist + section_im * cos_twist
    final_re = mixed('...cb,bd->...dc', twist_re, cos_second) - mixed('...cb,bd->...dc', twist_im, sin_second)
    final_im = mixed('...cb,bd->...dc', twist_re, sin_second) + mixed('...cb,bd->...dc', twist_im, cos_second)
    return final_re.reshape(shape_lead + (length,)), final_im.reshape(shape_lead + (length,))


def reference(intensity, punch_radius):
    coords = jnp.arange(N, dtype=jnp.int32)
    node_of = (coords + SP // 2) // SP
    offsets = coords - SP * node_of
    dist_sq = offsets[:, None] * offsets[:, None] + offsets[None, :] * offsets[None, :]

    def plane(inputs):
        levels, values = inputs
        plane_node = (levels + SP // 2) // SP
        plane_off = levels - SP * plane_node
        radius_plane = punch_radius[plane_node]
        radius = radius_plane[node_of[:, None], node_of[None, :]]
        keep_mask = (dist_sq + plane_off * plane_off >= radius).astype(jnp.float32)
        keep_swap = keep_mask.T
        counts = jnp.maximum(keep_mask + keep_swap, 1.0)
        symmetric = ((keep_mask * values + keep_swap * values.T) / counts).astype(jnp.bfloat16)
        part_re, part_im = spectral(symmetric.astype(jnp.float32), None)
        real_out, imag_out = spectral(part_re.T, part_im.T)
        return real_out / N, imag_out / N

    plane_ids = jnp.arange(L, dtype=jnp.int32)
    out_re, out_im = lax.map(plane, (plane_ids, intensity))
    return out_re, out_im
```

```python
import functools

import jax
import jax.numpy as jnp
import ml_dtypes
import numpy as np
from jax import lax
from jax.experimental import pallas as pl
from jax.experimental.pallas import tpu as pltpu
from jax.sharding import PartitionSpec as P

N = 2048
SP = 16
PLANES = 16
CLASSES = 16
OWN = N // CLASSES
LANES = 128
TOP = 6.0
CODE = 32700.0 / TOP**0.25
BF = jnp.bfloat16
F32 = jnp.float32


def dot(left, right, contract=(1, 0)):
    dims = (((contract[0],), (contract[1],)), ((), ()))
    return lax.dot_general(left, right, dims, preferred_element_type=F32)


def split_table(table):
    high = table.astype(ml_dtypes.bfloat16)
    low = (table - high.astype(np.float64)).astype(ml_dtypes.bfloat16)
    return high, low


def wave(phases, period):
    angles = 2.0 * np.pi * (phases % period) / period
    return np.cos(angles), np.sin(angles)


def encode_kernel(step_planes, at_ref, table_ref, x_ref, out_ref, g_ref, e_ref, t_ref):
    step = pl.program_id(0)
    half = LANES // 2

    @pl.when(step == 0)
    def _():
        row_at, col_at = at_ref[0], at_ref[1]
        rows = lax.broadcasted_iota(jnp.int32, (256, 256), 0)
        nodes = lax.broadcasted_iota(jnp.int32, (256, 256), 1)
        pick_h = ((256 * row_at + rows + SP // 2) // SP == nodes).astype(F32).astype(BF)
        sub = lax.broadcasted_iota(jnp.int32, (256, LANES), 0)
        lane = lax.broadcasted_iota(jnp.int32, (256, LANES), 1)
        same = (64 * col_at + lane % half + SP // 2) // SP == sub
        pick_low = (same & (lane < half)).astype(F32).astype(BF)
        pick_high = (same & (lane >= half)).astype(F32).astype(BF)
        off_h = (lax.broadcasted_iota(jnp.int32, (128, LANES), 0) + SP // 2) % SP - SP // 2
        off_k = (lax.broadcasted_iota(jnp.int32, (128, LANES), 1) + SP // 2) % SP - SP // 2
        near = (off_h * off_h + off_k * off_k).astype(F32)
        for s in range(2):
            for side in range(2):
                left = dot(pick_h, table_ref[s], (1, side)).astype(BF)
                radius = dot(left[:128], pick_low) + dot(left[128:], pick_high)
                g_ref[2 * s + side] = radius - near

    for i in range(step_planes):
        level = step * step_planes + i
        node = (level + SP // 2) // SP
        off = level - SP * node
        far = (off * off).astype(F32)
        x = x_ref[i]
        packed = jnp.concatenate([x[:128], x[128:]], axis=1)
        keep = far >= g_ref[2 * node]
        swap = far >= g_ref[2 * node + 1]
        value = jnp.where(keep, packed * jnp.where(swap, 0.5, 1.0), 0.0)
        size = lax.rsqrt(lax.rsqrt(jnp.abs(value))) * CODE + 0.5
        size = size.astype(jnp.int32)
        code = jnp.where(value < 0.0, -size, size)
        e_ref[i] = code
        t_ref[i] = code.T
        for m in range(CLASSES):
            direct = t_ref[i, pl.ds(m, 8, stride=CLASSES), :]
            mirror = e_ref[i, pl.ds(m, 8, stride=CLASSES), :]
            out_ref[i * CLASSES + m] = jnp.concatenate([direct, mirror], axis=0).astype(jnp.int16)


def encode(at, table, intensity):
    planes, h_block, k_block = intensity.shape
    step_planes = 4
    steps = planes // step_planes
    count = step_planes * CLASSES
    return pl.pallas_call(
        functools.partial(encode_kernel, step_planes),
        grid=(steps,),
        in_specs=[
            pl.BlockSpec(memory_space=pltpu.SMEM),
            pl.BlockSpec((2, 256, 256), lambda i: (0, 0, 0)),
            pl.BlockSpec((step_planes, h_block, k_block), lambda i: (i, 0, 0)),
        ],
        out_specs=pl.BlockSpec((count, 16, LANES), lambda i: (i, 0, 0)),
        out_shape=jax.ShapeDtypeStruct((planes * CLASSES, 16, LANES), jnp.int16),
        scratch_shapes=[
            pltpu.VMEM((4, 128, LANES), F32),
            pltpu.VMEM((step_planes, 128, LANES), jnp.int32),
            pltpu.VMEM((step_planes, 128, LANES), jnp.int32),
        ],
        compiler_params=pltpu.CompilerParams(vmem_limit_bytes=24 << 20),
    )(at, table, intensity)


def decoded(codes):
    u = codes.astype(jnp.int32).astype(F32) * (1.0 / CODE)
    return (u * u) * (u * jnp.abs(u))


def times(re, im, c, s):
    return re * c - im * s, re * s + im * c


def four(a, b, c, d):
    s_re, s_im = a[0] + c[0], a[1] + c[1]
    d_re, d_im = a[0] - c[0], a[1] - c[1]
    t_re, t_im = b[0] + d[0], b[1] + d[1]
    e_re, e_im = b[0] - d[0], b[1] - d[1]
    return (
        (s_re + t_re, s_im + t_im),
        (d_re - e_im, d_im + e_re),
        (s_re - t_re, s_im - t_im),
        (d_re + e_im, d_im - e_re),
    )


def eight(y):
    even = four(y[0], y[2], y[4], y[6])
    odd = four(y[1], y[3], y[5], y[7])
    root = float(np.sqrt(0.5))
    o1 = ((odd[1][0] - odd[1][1]) * root, (odd[1][0] + odd[1][1]) * root)
    o2 = (-odd[2][1], odd[2][0])
    o3 = (-(odd[3][0] + odd[3][1]) * root, (odd[3][0] - odd[3][1]) * root)
    odd = (odd[0], o1, o2, o3)
    first = [(e[0] + o[0], e[1] + o[1]) for e, o in zip(even, odd)]
    second = [(e[0] - o[0], e[1] - o[1]) for e, o in zip(even, odd)]
    return first + second


def column_kernel(codes_ref, dft_ref, cos_ref, sin_ref, out_ref, s_ref, y_ref):
    sub = lax.broadcasted_iota(jnp.int32, (16, 8, LANES), 1)
    lane = lax.broadcasted_iota(jnp.int32, (8, 8, LANES), 2)
    for tile in range(N // LANES):
        row, upper = tile // 2, tile % 2
        got = decoded(codes_ref[32 * row : 32 * row + 32])[:, :8].reshape(16, 2, 8, LANES)
        even, odd = got[:, 0], got[:, 1]
        if upper:
            direct = jnp.where(sub < 4, pltpu.roll(even, 4, 1), odd)
        else:
            direct = jnp.where(sub < 4, even, pltpu.roll(odd, 4, 1))
        pair = [
            jnp.stack([decoded(codes_ref[32 * r + 2 * tile + j])[8:] for r in range(8)])
            for j in range(2)
        ]
        low = jnp.where(lane < 64, pair[0], pltpu.roll(pair[1], 64, 2))
        high = jnp.where(lane < 64, pltpu.roll(pair[0], 64, 2), pair[1])
        mirror = jnp.stack([low, high], axis=1)
        whole = direct.reshape(128, LANES) + mirror.reshape(128, LANES)
        s_ref[tile * LANES : (tile + 1) * LANES, :] = whole.T
    right = jnp.concatenate(
        [s_ref[pl.ds(a, 256, stride=8), :].astype(BF) for a in range(8)], axis=1
    )
    y_ref[...] = dot(dft_ref[...], jnp.concatenate([right, right], axis=0))

    def block(i, carry):
        at = pl.multiple_of(i * 8, 8)
        y = []
        for a in range(8):
            lanes = slice(a * LANES, (a + 1) * LANES)
            re = y_ref[pl.ds(at, 8), lanes]
            im = y_ref[pl.ds(256 + at, 8), lanes]
            if a:
                re, im = times(re, im, cos_ref[pl.ds(at, 8), lanes], sin_ref[pl.ds(at, 8), lanes])
            y.append((re, im))
        for c, (re, im) in enumerate(eight(y)):
            out_ref[32 * c + i] = jnp.concatenate([re, im], axis=0).astype(BF)
        return carry

    lax.fori_loop(0, 32, block, 0)


def column_tables():
    d = np.arange(256)
    cos, sin = wave(d[:, None] * d[None, :], 256)
    high, low = split_table(np.concatenate([cos, sin], axis=0))
    dft = np.concatenate([high, low], axis=1)
    cos, sin = wave(d[:, None] * np.repeat(np.arange(8), LANES)[None, :], N)
    return dft, cos.astype(np.float32), sin.astype(np.float32)


def columns(codes):
    vmem = pl.BlockSpec(memory_space=pltpu.VMEM)
    return pl.pallas_call(
        column_kernel,
        in_specs=[vmem] * 4,
        out_specs=vmem,
        out_shape=jax.ShapeDtypeStruct((256, 16, LANES), BF),
        scratch_shapes=[pltpu.VMEM((N, LANES), F32), pltpu.VMEM((512, 8 * LANES), F32)],
        compiler_params=pltpu.CompilerParams(vmem_limit_bytes=40 << 20),
    )(codes, *map(jnp.asarray, column_tables()))


def sixteen(y):
    first = [four(y[i], y[i + 4], y[i + 8], y[i + 12]) for i in range(4)]
    out = [None] * 16
    for k in range(4):
        turned = []
        for i in range(4):
            re, im = first[i][k]
            if i * k:
                angle = 2.0 * np.pi * i * k / 16
                c, s = float(np.cos(angle)), float(np.sin(angle))
                if i * k == 4:
                    re, im = -im, re
                elif i * k == 2:
                    re, im = (re - im) * c, (re + im) * c
                elif i * k == 6:
                    re, im = -(re + im) * s, (re - im) * s
                else:
                    re, im = times(re, im, c, s)
            turned.append((re, im))
        for j, value in enumerate(four(*turned)):
            out[k + 4 * j] = value
    return out


def row_kernel(step_planes, x_ref, dft_ref, cos_ref, sin_ref, re_ref, im_ref, y_ref):
    for i in range(step_planes):
        x = x_ref[CLASSES * i : CLASSES * (i + 1)].reshape(CLASSES * 16, LANES)
        y_ref[i] = dot(jnp.concatenate([x, x], axis=1), dft_ref[...])
        y = []
        for m in range(CLASSES):
            real, imag = slice(16 * m, 16 * m + 8), slice(16 * m + 8, 16 * m + 16)
            re = y_ref[i, real, :LANES] - y_ref[i, imag, LANES:]
            im = y_ref[i, real, LANES:] + y_ref[i, imag, :LANES]
            if m:
                re, im = times(re, im, cos_ref[m : m + 1], sin_ref[m : m + 1])
            y.append((re, im))
        for d, (re, im) in enumerate(sixteen(y)):
            re_ref[i, :, d * LANES : (d + 1) * LANES] = re
            im_ref[i, :, d * LANES : (d + 1) * LANES] = im


def row_tables():
    t = np.arange(LANES)
    cos, sin = wave(t[:, None] * t[None, :], LANES)
    high, low = split_table(np.concatenate([cos, sin], axis=1) / N)
    cos, sin = wave(np.arange(CLASSES)[:, None] * t[None, :], N)
    return np.concatenate([high, low], axis=0), cos.astype(np.float32), sin.astype(np.float32)


def rows(spectra):
    step_planes = 4
    block = pl.BlockSpec((step_planes, 8, N), lambda i: (i, 0, 0))
    shape = jax.ShapeDtypeStruct((PLANES, 8, N), F32)
    return pl.pallas_call(
        functools.partial(row_kernel, step_planes),
        grid=(PLANES // step_planes,),
        in_specs=[
            pl.BlockSpec((step_planes * CLASSES, 16, LANES), lambda i: (i, 0, 0)),
            pl.BlockSpec((2 * LANES, 2 * LANES), lambda i: (0, 0)),
            pl.BlockSpec((CLASSES, LANES), lambda i: (0, 0)),
            pl.BlockSpec((CLASSES, LANES), lambda i: (0, 0)),
        ],
        out_specs=[block, block],
        out_shape=[shape, shape],
        scratch_shapes=[pltpu.VMEM((step_planes, 256, 256), F32)],
        compiler_params=pltpu.CompilerParams(vmem_limit_bytes=40 << 20),
    )(spectra, *map(jnp.asarray, row_tables()))


def exchange(array):
    return lax.all_to_all(array, ("row", "col"), split_axis=0, concat_axis=0, tiled=True)


def body(intensity, punch_radius):
    at = jnp.stack([lax.axis_index("row"), lax.axis_index("col")]).astype(jnp.int32)
    nodes = punch_radius.shape[1]
    table = jnp.pad(punch_radius.astype(BF), ((0, 0), (0, 256 - nodes), (0, 256 - nodes)))
    codes = exchange(encode(at, table, intensity))
    spectra = exchange(columns(codes))
    return tuple(rows(spectra))


def solution(mesh):
    in_specs = (P(None, "row", "col"), P())
    out_specs = (P(None, ("row", "col"), None), P(None, ("row", "col"), None))
    return jax.shard_map(body, mesh=mesh, in_specs=in_specs, out_specs=out_specs, check_vma=False)
```

```python
import jax
import jax.numpy as jnp
import ml_dtypes
import numpy as np
from jax import lax
from jax.experimental import pallas as pl
from jax.experimental.pallas import tpu as pltpu
from jax.sharding import PartitionSpec as P

N = 2048
SP = 16
PLANES = 16
CLASSES = 16
OWN = N // CLASSES
LANES = 128
TOP = 6.0
CODE = 32700.0 / TOP**0.25
BF = jnp.bfloat16
F32 = jnp.float32


def dot(left, right, contract=(1, 0)):
    dims = (((contract[0],), (contract[1],)), ((), ()))
    return lax.dot_general(left, right, dims, preferred_element_type=F32)


def split_table(table):
    high = table.astype(ml_dtypes.bfloat16)
    low = (table - high.astype(np.float64)).astype(ml_dtypes.bfloat16)
    return high, low


def wave(phases, period):
    angles = 2.0 * np.pi * (phases % period) / period
    return np.cos(angles), np.sin(angles)


def encode_kernel(x_hbm, table_hbm, out_hbm, code_ref, x_ref, near_h, near_k, g_ref, e_ref, t_ref, sems):
    half = LANES // 2
    row_at, col_at = lax.axis_index("row"), lax.axis_index("col")
    across, down = near_h.shape[0], near_k.shape[0]
    tables = [
        pltpu.make_async_copy(table_hbm.at[pl.ds(16 * row_at, across)], near_h, sems.at[4]),
        pltpu.make_async_copy(table_hbm.at[pl.ds(4 * col_at, down)], near_k, sems.at[5]),
    ]
    chunks = [
        pltpu.make_async_copy(x_hbm.at[pl.ds(4 * j, 4)], x_ref.at[pl.ds(4 * j, 4)], sems.at[j])
        for j in range(4)
    ]
    for copy in tables + chunks:
        copy.start()

    def picks(shape, base):
        places = lax.broadcasted_iota(jnp.int32, shape, 0)
        nodes = lax.broadcasted_iota(jnp.int32, shape, 1)
        return ((base + places + SP // 2) // SP == nodes).astype(F32).astype(BF)

    h_any, k_any = picks((256, table_hbm.shape[2]), 256 * row_at), picks((64, table_hbm.shape[2]), 64 * col_at)
    h_own, k_own = picks((256, across), 0), picks((64, down), 0)
    off_h = (lax.broadcasted_iota(jnp.int32, (64, 256), 1) + SP // 2) % SP - SP // 2
    off_k = (lax.broadcasted_iota(jnp.int32, (64, 256), 0) + SP // 2) % SP - SP // 2
    near = (off_h * off_h + off_k * off_k).astype(F32)
    for copy in tables:
        copy.wait()
    for s in range(2):
        keep = dot(k_any, near_h[:, s, :].astype(F32).astype(BF), (1, 1)).astype(BF)
        keep = dot(keep, h_own, (1, 1)) - near
        swap = dot(k_own, near_k[:, s, :].astype(F32).astype(BF)).astype(BF)
        swap = dot(swap, h_any, (1, 1)) - near
        for side, g in enumerate((keep, swap)):
            g_ref[2 * s + side] = jnp.concatenate([g[:, :128], g[:, 128:]], axis=0)

    def plane(level, node, far):
        x = x_ref[level]
        packed = jnp.concatenate([x[:, :128], x[:, 128:]], axis=0)
        keep = far >= g_ref[2 * node]
        swap = far >= g_ref[2 * node + 1]
        value = jnp.where(keep, packed * jnp.where(swap, 0.5, 1.0), 0.0)
        size = lax.rsqrt(lax.rsqrt(jnp.abs(value))) * CODE + 0.5
        size = size.astype(jnp.int32)
        code = jnp.where(value < 0.0, -size, size)
        t_ref[level] = code
        e_ref[level] = code.T
        for m in range(CLASSES):
            direct = t_ref[level, pl.ds(m, 8, stride=CLASSES), :]
            mirror = e_ref[level, pl.ds(m, 8, stride=CLASSES), :]
            both = jnp.concatenate([direct, mirror], axis=0).astype(jnp.int16)
            code_ref[level * CLASSES + m] = both

    sent = []
    for j in range(4):
        chunks[j].wait()
        for level in range(4 * j, 4 * j + 4):
            node = (level + SP // 2) // SP
            plane(level, node, float((level - SP * node) ** 2))
        part = pl.ds(4 * CLASSES * j, 4 * CLASSES)
        copy = pltpu.make_async_copy(code_ref.at[part], out_hbm.at[part], sems.at[6 + j])
        copy.start()
        sent.append(copy)
    for copy in sent:
        copy.wait()


def encode(intensity, punch_radius):
    planes, h_block, k_block = intensity.shape
    hbm = pl.BlockSpec(memory_space=pltpu.HBM)
    across, down, nodes = h_block // SP + 1, k_block // SP + 1, punch_radius.shape[2]
    return pl.pallas_call(
        encode_kernel,
        in_specs=[hbm, hbm],
        out_specs=hbm,
        out_shape=jax.ShapeDtypeStruct((planes * CLASSES, 16, LANES), jnp.int16),
        scratch_shapes=[
            pltpu.VMEM((planes * CLASSES, 16, LANES), jnp.int16),
            pltpu.VMEM((planes, k_block, h_block), F32),
            pltpu.VMEM((across, 2, nodes), jnp.int32),
            pltpu.VMEM((down, 2, nodes), jnp.int32),
            pltpu.VMEM((4, 128, LANES), F32),
            pltpu.VMEM((planes, 128, LANES), jnp.int32),
            pltpu.VMEM((planes, 128, LANES), jnp.int32),
            pltpu.SemaphoreType.DMA((10,)),
        ],
        compiler_params=pltpu.CompilerParams(vmem_limit_bytes=58 << 20),
    )(jnp.swapaxes(intensity, 1, 2), jnp.swapaxes(punch_radius, 0, 1))


def decoded(codes):
    u = codes.astype(jnp.int32).astype(F32) * (1.0 / CODE)
    return (u * u) * (u * jnp.abs(u))


def times(re, im, c, s):
    return re * c - im * s, re * s + im * c


def four(a, b, c, d):
    s_re, s_im = a[0] + c[0], a[1] + c[1]
    d_re, d_im = a[0] - c[0], a[1] - c[1]
    t_re, t_im = b[0] + d[0], b[1] + d[1]
    e_re, e_im = b[0] - d[0], b[1] - d[1]
    return (
        (s_re + t_re, s_im + t_im),
        (d_re - e_im, d_im + e_re),
        (s_re - t_re, s_im - t_im),
        (d_re + e_im, d_im - e_re),
    )


def eight(y):
    even = four(y[0], y[2], y[4], y[6])
    odd = four(y[1], y[3], y[5], y[7])
    root = float(np.sqrt(0.5))
    o1 = ((odd[1][0] - odd[1][1]) * root, (odd[1][0] + odd[1][1]) * root)
    o2 = (-odd[2][1], odd[2][0])
    o3 = (-(odd[3][0] + odd[3][1]) * root, (odd[3][0] - odd[3][1]) * root)
    odd = (odd[0], o1, o2, o3)
    first = [(e[0] + o[0], e[1] + o[1]) for e, o in zip(even, odd)]
    second = [(e[0] - o[0], e[1] - o[1]) for e, o in zip(even, odd)]
    return first + second


def column_kernel(codes_ref, order_ref, dft_ref, cos_ref, sin_ref, out_ref, s_ref, y_ref):
    sub = lax.broadcasted_iota(jnp.int32, (16, 8, LANES), 1)
    lane = lax.broadcasted_iota(jnp.int32, (8, 8, LANES), 2)
    for tile in range(N // LANES):
        row, upper = tile // 2, tile % 2
        got = decoded(codes_ref[32 * row : 32 * row + 32])[:, :8].reshape(16, 2, 8, LANES)
        even, odd = got[:, 0], got[:, 1]
        if upper:
            direct = jnp.where(sub < 4, pltpu.roll(even, 4, 1), odd)
        else:
            direct = jnp.where(sub < 4, even, pltpu.roll(odd, 4, 1))
        pair = [
            jnp.stack([decoded(codes_ref[32 * r + 2 * tile + j])[8:] for r in range(8)])
            for j in range(2)
        ]
        low = jnp.where(lane < 64, pair[0], pltpu.roll(pair[1], 64, 2))
        high = jnp.where(lane < 64, pltpu.roll(pair[0], 64, 2), pair[1])
        mirror = jnp.stack([low, high], axis=1)
        whole = (direct.reshape(128, LANES) + mirror.reshape(128, LANES)).astype(BF)
        turned = dot(order_ref[...], whole, (1, 1)).astype(BF)
        for a in range(8):
            lanes = slice(a * LANES, (a + 1) * LANES)
            s_ref[16 * tile : 16 * tile + 16, lanes] = turned[16 * a : 16 * a + 16]
    right = s_ref[...]
    right = jnp.concatenate([right, right], axis=0)
    for part in range(2):
        y_ref[256 * part : 256 * part + 256] = dot(dft_ref[256 * part : 256 * part + 256], right)
    for i in range(32):
        y = []
        for a in range(8):
            lanes = slice(a * LANES, (a + 1) * LANES)
            at = slice(8 * i, 8 * i + 8)
            here = 8 * i + i // 16 * 128
            re, im = y_ref[here : here + 8, lanes], y_ref[here + 128 : here + 136, lanes]
            if a:
                re, im = times(re, im, cos_ref[at, lanes], sin_ref[at, lanes])
            y.append((re, im))
        for c, (re, im) in enumerate(eight(y)):
            out_ref[32 * c + i] = jnp.concatenate([re, im], axis=0).astype(BF)


def column_tables():
    d = np.arange(256)
    cos, sin = wave(d[:, None] * d[None, :], 256)
    order = [cos[:128], sin[:128], cos[128:], sin[128:]]
    high, low = split_table(np.concatenate(order, axis=0))
    dft = np.concatenate([high, low], axis=1)
    cos, sin = wave(d[:, None] * np.repeat(np.arange(8), LANES)[None, :], N)
    order = np.zeros((LANES, LANES))
    order[np.arange(LANES), np.arange(LANES) % 16 * 8 + np.arange(LANES) // 16] = 1.0
    return order.astype(ml_dtypes.bfloat16), dft, cos.astype(np.float32), sin.astype(np.float32)


def columns(codes):
    vmem = pl.BlockSpec(memory_space=pltpu.VMEM)
    return pl.pallas_call(
        column_kernel,
        in_specs=[vmem] * 5,
        out_specs=vmem,
        out_shape=jax.ShapeDtypeStruct((256, 16, LANES), BF),
        scratch_shapes=[pltpu.VMEM((256, 8 * LANES), BF), pltpu.VMEM((512, 8 * LANES), F32)],
        compiler_params=pltpu.CompilerParams(vmem_limit_bytes=40 << 20),
    )(codes, *map(jnp.asarray, column_tables()))


def sixteen(y):
    first = [four(y[i], y[i + 4], y[i + 8], y[i + 12]) for i in range(4)]
    out = [None] * 16
    for k in range(4):
        turned = []
        for i in range(4):
            re, im = first[i][k]
            if i * k:
                angle = 2.0 * np.pi * i * k / 16
                c, s = float(np.cos(angle)), float(np.sin(angle))
                if i * k == 4:
                    re, im = -im, re
                elif i * k == 2:
                    re, im = (re - im) * c, (re + im) * c
                elif i * k == 6:
                    re, im = -(re + im) * s, (re - im) * s
                else:
                    re, im = times(re, im, c, s)
            turned.append((re, im))
        for j, value in enumerate(four(*turned)):
            out[k + 4 * j] = value
    return out


def row_kernel(x_ref, dft_ref, cos_ref, sin_ref, re_hbm, im_hbm, re_ref, im_ref, y_ref, sems):
    copies = []

    def matmul(i):
        x = x_ref[CLASSES * i : CLASSES * (i + 1)].reshape(CLASSES * 16, LANES)
        y_ref[i] = dot(jnp.concatenate([x, x], axis=1), dft_ref[...])

    matmul(0)
    for i in range(PLANES):
        if i + 1 < PLANES:
            matmul(i + 1)
        y = []
        for m in range(CLASSES):
            real, imag = slice(16 * m, 16 * m + 8), slice(16 * m + 8, 16 * m + 16)
            re = y_ref[i, real, :LANES] - y_ref[i, imag, LANES:]
            im = y_ref[i, real, LANES:] + y_ref[i, imag, :LANES]
            if m:
                re, im = times(re, im, cos_ref[m : m + 1], sin_ref[m : m + 1])
            y.append((re, im))
        for d, (re, im) in enumerate(sixteen(y)):
            re_ref[i, :, d * LANES : (d + 1) * LANES] = re
            im_ref[i, :, d * LANES : (d + 1) * LANES] = im
        if i % 2:
            done = pl.ds(i - 1, 2)
            pairs = ((re_ref, re_hbm), (im_ref, im_hbm))
            for which, (here, there) in enumerate(pairs):
                copy = pltpu.make_async_copy(here.at[done], there.at[done], sems.at[i // 2, which])
                copy.start()
                copies.append(copy)
    for copy in copies:
        copy.wait()


def row_tables():
    t = np.arange(LANES)
    cos, sin = wave(t[:, None] * t[None, :], LANES)
    high, low = split_table(np.concatenate([cos, sin], axis=1) / N)
    cos, sin = wave(np.arange(CLASSES)[:, None] * t[None, :], N)
    return np.concatenate([high, low], axis=0), cos.astype(np.float32), sin.astype(np.float32)


def rows(spectra):
    vmem, hbm = pl.BlockSpec(memory_space=pltpu.VMEM), pl.BlockSpec(memory_space=pltpu.HBM)
    shape = jax.ShapeDtypeStruct((PLANES, 8, N), F32)
    return pl.pallas_call(
        row_kernel,
        in_specs=[vmem] * 4,
        out_specs=[hbm, hbm],
        out_shape=[shape, shape],
        scratch_shapes=[
            pltpu.VMEM((PLANES, 8, N), F32),
            pltpu.VMEM((PLANES, 8, N), F32),
            pltpu.VMEM((PLANES, 256, 256), F32),
            pltpu.SemaphoreType.DMA((PLANES // 2, 2)),
        ],
        compiler_params=pltpu.CompilerParams(vmem_limit_bytes=40 << 20),
    )(spectra, *map(jnp.asarray, row_tables()))


def exchange(array):
    return lax.all_to_all(array, ("row", "col"), split_axis=0, concat_axis=0, tiled=True)


def body(intensity, punch_radius):
    codes = exchange(encode(intensity, punch_radius))
    spectra = exchange(columns(codes))
    return tuple(rows(spectra))


def solution(mesh):
    in_specs = (P(None, "row", "col"), P())
    out_specs = (P(None, ("row", "col"), None), P(None, ("row", "col"), None))
    return jax.shard_map(body, mesh=mesh, in_specs=in_specs, out_specs=out_specs, check_vma=False)
```

```python
import jax
import jax.numpy as jnp
import ml_dtypes
import numpy as np
from jax import lax
from jax.experimental import pallas as pl
from jax.experimental.pallas import tpu as pltpu
from jax.sharding import PartitionSpec as P

N = 2048
SP = 16
PLANES = 16
CLASSES = 16
OWN = N // CLASSES
LANES = 128
TOP = 6.0
CODE = 32700.0 / TOP**0.25
BF = jnp.bfloat16
F32 = jnp.float32


def dot(left, right, contract=(1, 0)):
    dims = (((contract[0],), (contract[1],)), ((), ()))
    return lax.dot_general(left, right, dims, preferred_element_type=F32)


def split_table(table):
    high = table.astype(ml_dtypes.bfloat16)
    low = (table - high.astype(np.float64)).astype(ml_dtypes.bfloat16)
    return high, low


def wave(phases, period):
    angles = 2.0 * np.pi * (phases % period) / period
    return np.cos(angles), np.sin(angles)


def encode_kernel(x_hbm, table_hbm, code_ref, x_ref, near_h, near_k, g_ref, e_ref, t_ref, sems):
    half = LANES // 2
    row_at, col_at = lax.axis_index("row"), lax.axis_index("col")
    across, down = near_h.shape[0], near_k.shape[0]
    tables = [
        pltpu.make_async_copy(table_hbm.at[pl.ds(16 * row_at, across)], near_h, sems.at[4]),
        pltpu.make_async_copy(table_hbm.at[pl.ds(4 * col_at, down)], near_k, sems.at[5]),
    ]
    chunks = [
        pltpu.make_async_copy(x_hbm.at[pl.ds(4 * j, 4)], x_ref.at[pl.ds(4 * j, 4)], sems.at[j])
        for j in range(4)
    ]
    for copy in tables + chunks:
        copy.start()

    def picks(shape, base):
        places = lax.broadcasted_iota(jnp.int32, shape, 0)
        nodes = lax.broadcasted_iota(jnp.int32, shape, 1)
        return ((base + places + SP // 2) // SP == nodes).astype(F32).astype(BF)

    h_any, k_any = picks((256, table_hbm.shape[2]), 256 * row_at), picks((64, table_hbm.shape[2]), 64 * col_at)
    h_own, k_own = picks((256, across), 0), picks((64, down), 0)
    off_h = (lax.broadcasted_iota(jnp.int32, (64, 256), 1) + SP // 2) % SP - SP // 2
    off_k = (lax.broadcasted_iota(jnp.int32, (64, 256), 0) + SP // 2) % SP - SP // 2
    near = (off_h * off_h + off_k * off_k).astype(F32)
    for copy in tables:
        copy.wait()
    for s in range(2):
        keep = dot(k_any, near_h[:, s, :].astype(F32).astype(BF), (1, 1)).astype(BF)
        keep = dot(keep, h_own, (1, 1)) - near
        swap = dot(k_own, near_k[:, s, :].astype(F32).astype(BF)).astype(BF)
        swap = dot(swap, h_any, (1, 1)) - near
        for side, g in enumerate((keep, swap)):
            g_ref[2 * s + side] = jnp.concatenate([g[:, :128], g[:, 128:]], axis=0)

    def plane(level, node, far):
        x = x_ref[level]
        packed = jnp.concatenate([x[:, :128], x[:, 128:]], axis=0)
        keep = far >= g_ref[2 * node]
        swap = far >= g_ref[2 * node + 1]
        value = jnp.where(keep, packed * jnp.where(swap, 0.5, 1.0), 0.0)
        size = lax.rsqrt(lax.rsqrt(jnp.abs(value))) * CODE + 0.5
        size = size.astype(jnp.int32)
        code = jnp.where(value < 0.0, -size, size)
        t_ref[level] = code
        e_ref[level] = code.T
        for m in range(CLASSES):
            direct = t_ref[level, pl.ds(m, 8, stride=CLASSES), :]
            mirror = e_ref[level, pl.ds(m, 8, stride=CLASSES), :]
            both = jnp.concatenate([direct, mirror], axis=0).astype(jnp.int16)
            code_ref[level * CLASSES + m] = both

    for j in range(4):
        chunks[j].wait()
        for level in range(4 * j, 4 * j + 4):
            node = (level + SP // 2) // SP
            plane(level, node, float((level - SP * node) ** 2))


def encode(intensity, punch_radius):
    planes, h_block, k_block = intensity.shape
    hbm = pl.BlockSpec(memory_space=pltpu.HBM)
    across, down, nodes = h_block // SP + 1, k_block // SP + 1, punch_radius.shape[2]
    return pl.pallas_call(
        encode_kernel,
        in_specs=[hbm, hbm],
        out_specs=pl.BlockSpec(memory_space=pltpu.VMEM),
        out_shape=pltpu.VMEM((planes * CLASSES, 16, LANES), jnp.int16),
        scratch_shapes=[
            pltpu.VMEM((planes, k_block, h_block), F32),
            pltpu.VMEM((across, 2, nodes), jnp.int32),
            pltpu.VMEM((down, 2, nodes), jnp.int32),
            pltpu.VMEM((4, 128, LANES), F32),
            pltpu.VMEM((planes, 128, LANES), jnp.int32),
            pltpu.VMEM((planes, 128, LANES), jnp.int32),
            pltpu.SemaphoreType.DMA((6,)),
        ],
        compiler_params=pltpu.CompilerParams(vmem_limit_bytes=58 << 20),
    )(jnp.swapaxes(intensity, 1, 2), jnp.swapaxes(punch_radius, 0, 1))


def decoded(codes):
    u = codes.astype(jnp.int32).astype(F32) * (1.0 / CODE)
    return (u * u) * (u * jnp.abs(u))


def times(re, im, c, s):
    return re * c - im * s, re * s + im * c


def four(a, b, c, d):
    s_re, s_im = a[0] + c[0], a[1] + c[1]
    d_re, d_im = a[0] - c[0], a[1] - c[1]
    t_re, t_im = b[0] + d[0], b[1] + d[1]
    e_re, e_im = b[0] - d[0], b[1] - d[1]
    return (
        (s_re + t_re, s_im + t_im),
        (d_re - e_im, d_im + e_re),
        (s_re - t_re, s_im - t_im),
        (d_re + e_im, d_im - e_re),
    )


def eight(y):
    even = four(y[0], y[2], y[4], y[6])
    odd = four(y[1], y[3], y[5], y[7])
    root = float(np.sqrt(0.5))
    o1 = ((odd[1][0] - odd[1][1]) * root, (odd[1][0] + odd[1][1]) * root)
    o2 = (-odd[2][1], odd[2][0])
    o3 = (-(odd[3][0] + odd[3][1]) * root, (odd[3][0] - odd[3][1]) * root)
    odd = (odd[0], o1, o2, o3)
    first = [(e[0] + o[0], e[1] + o[1]) for e, o in zip(even, odd)]
    second = [(e[0] - o[0], e[1] - o[1]) for e, o in zip(even, odd)]
    return first + second


def column_kernel(codes_ref, order_ref, dft_ref, cos_ref, sin_ref, out_ref, s_ref, y_ref):
    sub = lax.broadcasted_iota(jnp.int32, (16, 8, LANES), 1)
    lane = lax.broadcasted_iota(jnp.int32, (8, 8, LANES), 2)
    for tile in range(N // LANES):
        row, upper = tile // 2, tile % 2
        got = decoded(codes_ref[32 * row : 32 * row + 32])[:, :8].reshape(16, 2, 8, LANES)
        even, odd = got[:, 0], got[:, 1]
        if upper:
            direct = jnp.where(sub < 4, pltpu.roll(even, 4, 1), odd)
        else:
            direct = jnp.where(sub < 4, even, pltpu.roll(odd, 4, 1))
        pair = [
            jnp.stack([decoded(codes_ref[32 * r + 2 * tile + j])[8:] for r in range(8)])
            for j in range(2)
        ]
        low = jnp.where(lane < 64, pair[0], pltpu.roll(pair[1], 64, 2))
        high = jnp.where(lane < 64, pltpu.roll(pair[0], 64, 2), pair[1])
        mirror = jnp.stack([low, high], axis=1)
        whole = (direct.reshape(128, LANES) + mirror.reshape(128, LANES)).astype(BF)
        turned = dot(order_ref[...], whole, (1, 1)).astype(BF)
        for a in range(8):
            lanes = slice(a * LANES, (a + 1) * LANES)
            s_ref[16 * tile : 16 * tile + 16, lanes] = turned[16 * a : 16 * a + 16]
    right = s_ref[...]
    right = jnp.concatenate([right, right], axis=0)
    for part in range(2):
        y_ref[256 * part : 256 * part + 256] = dot(dft_ref[256 * part : 256 * part + 256], right)
    for i in range(32):
        y = []
        for a in range(8):
            lanes = slice(a * LANES, (a + 1) * LANES)
            at = slice(8 * i, 8 * i + 8)
            here = 8 * i + i // 16 * 128
            re, im = y_ref[here : here + 8, lanes], y_ref[here + 128 : here + 136, lanes]
            if a:
                re, im = times(re, im, cos_ref[at, lanes], sin_ref[at, lanes])
            y.append((re, im))
        for c, (re, im) in enumerate(eight(y)):
            out_ref[32 * c + i] = jnp.concatenate([re, im], axis=0).astype(BF)


def column_tables():
    d = np.arange(256)
    cos, sin = wave(d[:, None] * d[None, :], 256)
    order = [cos[:128], sin[:128], cos[128:], sin[128:]]
    high, low = split_table(np.concatenate(order, axis=0))
    dft = np.concatenate([high, low], axis=1)
    cos, sin = wave(d[:, None] * np.repeat(np.arange(8), LANES)[None, :], N)
    order = np.zeros((LANES, LANES))
    order[np.arange(LANES), np.arange(LANES) % 16 * 8 + np.arange(LANES) // 16] = 1.0
    return order.astype(ml_dtypes.bfloat16), dft, cos.astype(np.float32), sin.astype(np.float32)


def columns(codes):
    vmem = pl.BlockSpec(memory_space=pltpu.VMEM)
    return pl.pallas_call(
        column_kernel,
        in_specs=[vmem] * 5,
        out_specs=vmem,
        out_shape=jax.ShapeDtypeStruct((256, 16, LANES), BF),
        scratch_shapes=[pltpu.VMEM((256, 8 * LANES), BF), pltpu.VMEM((512, 8 * LANES), F32)],
        compiler_params=pltpu.CompilerParams(vmem_limit_bytes=40 << 20),
    )(codes, *map(jnp.asarray, column_tables()))


def sixteen(y):
    first = [four(y[i], y[i + 4], y[i + 8], y[i + 12]) for i in range(4)]
    out = [None] * 16
    for k in range(4):
        turned = []
        for i in range(4):
            re, im = first[i][k]
            if i * k:
                angle = 2.0 * np.pi * i * k / 16
                c, s = float(np.cos(angle)), float(np.sin(angle))
                if i * k == 4:
                    re, im = -im, re
                elif i * k == 2:
                    re, im = (re - im) * c, (re + im) * c
                elif i * k == 6:
                    re, im = -(re + im) * s, (re - im) * s
                else:
                    re, im = times(re, im, c, s)
            turned.append((re, im))
        for j, value in enumerate(four(*turned)):
            out[k + 4 * j] = value
    return out


def row_kernel(x_ref, dft_ref, cos_ref, sin_ref, re_hbm, im_hbm, re_ref, im_ref, y_ref, sems):
    copies = []

    def matmul(i):
        x = x_ref[CLASSES * i : CLASSES * (i + 1)].astype(F32)
        real = x[:, :8].reshape(CLASSES * 8, LANES).astype(BF)
        imag = x[:, 8:].reshape(CLASSES * 8, LANES).astype(BF)
        y_ref[i] = dot(jnp.concatenate([real, imag, real, imag], axis=1), dft_ref[...])

    matmul(0)
    for i in range(PLANES):
        if i + 1 < PLANES:
            matmul(i + 1)
        y = []
        for m in range(CLASSES):
            re, im = y_ref[i, 8 * m : 8 * m + 8, :LANES], y_ref[i, 8 * m : 8 * m + 8, LANES:]
            if m:
                re, im = times(re, im, cos_ref[m : m + 1], sin_ref[m : m + 1])
            y.append((re, im))
        for d, (re, im) in enumerate(sixteen(y)):
            re_ref[i, :, d * LANES : (d + 1) * LANES] = re
            im_ref[i, :, d * LANES : (d + 1) * LANES] = im
        if i % 2:
            done = pl.ds(i - 1, 2)
            pairs = ((re_ref, re_hbm), (im_ref, im_hbm))
            for which, (here, there) in enumerate(pairs):
                copy = pltpu.make_async_copy(here.at[done], there.at[done], sems.at[i // 2, which])
                copy.start()
                copies.append(copy)
    for copy in copies:
        copy.wait()


def row_tables():
    t = np.arange(LANES)
    cos, sin = wave(t[:, None] * t[None, :], LANES)
    both = [np.concatenate([cos, sin], axis=1), np.concatenate([-sin, cos], axis=1)]
    high, low = split_table(np.concatenate(both, axis=0) / N)
    cos, sin = wave(np.arange(CLASSES)[:, None] * t[None, :], N)
    return np.concatenate([high, low], axis=0), cos.astype(np.float32), sin.astype(np.float32)


def rows(spectra):
    vmem, hbm = pl.BlockSpec(memory_space=pltpu.VMEM), pl.BlockSpec(memory_space=pltpu.HBM)
    shape = jax.ShapeDtypeStruct((PLANES, 8, N), F32)
    return pl.pallas_call(
        row_kernel,
        in_specs=[vmem] * 4,
        out_specs=[hbm, hbm],
        out_shape=[shape, shape],
        scratch_shapes=[
            pltpu.VMEM((PLANES, 8, N), F32),
            pltpu.VMEM((PLANES, 8, N), F32),
            pltpu.VMEM((PLANES, 128, 256), F32),
            pltpu.SemaphoreType.DMA((PLANES // 2, 2)),
        ],
        compiler_params=pltpu.CompilerParams(vmem_limit_bytes=40 << 20),
    )(spectra, *map(jnp.asarray, row_tables()))


def exchange(array):
    return lax.all_to_all(array, ("row", "col"), split_axis=0, concat_axis=0, tiled=True)


def body(intensity, punch_radius):
    codes = exchange(encode(intensity, punch_radius))
    spectra = exchange(columns(codes))
    return tuple(rows(spectra))


def solution(mesh):
    in_specs = (P(None, "row", "col"), P())
    out_specs = (P(None, ("row", "col"), None), P(None, ("row", "col"), None))
    return jax.shard_map(body, mesh=mesh, in_specs=in_specs, out_specs=out_specs, check_vma=False)
```

```python
import jax
import jax.numpy as jnp
import ml_dtypes
import numpy as np
from jax import lax
from jax.experimental import pallas as pl
from jax.experimental.pallas import tpu as pltpu
from jax.sharding import PartitionSpec as P

N = 2048
SP = 16
PLANES = 16
CLASSES = 16
OWN = N // CLASSES
LANES = 128
TOP = 6.0
CODE = 32700.0 / TOP**0.25
BF = jnp.bfloat16
F32 = jnp.float32


def dot(left, right, contract=(1, 0)):
    dims = (((contract[0],), (contract[1],)), ((), ()))
    return lax.dot_general(left, right, dims, preferred_element_type=F32)


def split_table(table):
    high = table.astype(ml_dtypes.bfloat16)
    low = (table - high.astype(np.float64)).astype(ml_dtypes.bfloat16)
    return high, low


def wave(phases, period):
    angles = 2.0 * np.pi * (phases % period) / period
    return np.cos(angles), np.sin(angles)


def encode_kernel(x_hbm, table_hbm, code_ref, x_ref, near_h, near_k, g_ref, e_ref, t_ref, sems):
    half = LANES // 2
    row_at, col_at = lax.axis_index("row"), lax.axis_index("col")
    across, down = near_h.shape[0], near_k.shape[0]
    tables = [
        pltpu.make_async_copy(table_hbm.at[pl.ds(16 * row_at, across)], near_h, sems.at[4]),
        pltpu.make_async_copy(table_hbm.at[pl.ds(4 * col_at, down)], near_k, sems.at[5]),
    ]
    chunks = [
        pltpu.make_async_copy(x_hbm.at[pl.ds(4 * j, 4)], x_ref.at[pl.ds(4 * j, 4)], sems.at[j])
        for j in range(4)
    ]
    for copy in tables + chunks:
        copy.start()

    def picks(shape, base):
        places = lax.broadcasted_iota(jnp.int32, shape, 0)
        nodes = lax.broadcasted_iota(jnp.int32, shape, 1)
        return ((base + places + SP // 2) // SP == nodes).astype(F32).astype(BF)

    h_any, k_any = picks((256, table_hbm.shape[2]), 256 * row_at), picks((64, table_hbm.shape[2]), 64 * col_at)
    h_own, k_own = picks((256, across), 0), picks((64, down), 0)
    off_h = (lax.broadcasted_iota(jnp.int32, (64, 256), 1) + SP // 2) % SP - SP // 2
    off_k = (lax.broadcasted_iota(jnp.int32, (64, 256), 0) + SP // 2) % SP - SP // 2
    near = (off_h * off_h + off_k * off_k).astype(F32)
    for copy in tables:
        copy.wait()
    for s in range(2):
        keep = dot(k_any, near_h[:, s, :].astype(F32).astype(BF), (1, 1)).astype(BF)
        keep = dot(keep, h_own, (1, 1)) - near
        swap = dot(k_own, near_k[:, s, :].astype(F32).astype(BF)).astype(BF)
        swap = dot(swap, h_any, (1, 1)) - near
        for side, g in enumerate((keep, swap)):
            g_ref[2 * s + side] = jnp.concatenate([g[:, :128], g[:, 128:]], axis=0)

    def coded(level):
        node = (level + SP // 2) // SP
        far = float((level - SP * node) ** 2)
        x = x_ref[level]
        packed = jnp.concatenate([x[:, :128], x[:, 128:]], axis=0)
        keep = far >= g_ref[2 * node]
        swap = far >= g_ref[2 * node + 1]
        value = jnp.where(keep, packed * jnp.where(swap, 0.5, 1.0), 0.0)
        size = lax.rsqrt(lax.rsqrt(jnp.abs(value))) * CODE + 0.5
        size = size.astype(jnp.int32)
        return jnp.where(value < 0.0, -size, size)

    for pair in range(PLANES // 2):
        if pair % 2 == 0:
            chunks[pair // 2].wait()
        word = (coded(2 * pair) << 16) | (coded(2 * pair + 1) & 0xFFFF)
        t_ref[pair] = word
        e_ref[pair] = word.T
        for m in range(CLASSES):
            direct = t_ref[pair, pl.ds(m, 8, stride=CLASSES), :]
            mirror = e_ref[pair, pl.ds(m, 8, stride=CLASSES), :]
            both = jnp.concatenate([direct, mirror], axis=0)
            code_ref[2 * pair * CLASSES + m] = (both >> 16).astype(jnp.int16)
            code_ref[(2 * pair + 1) * CLASSES + m] = ((both << 16) >> 16).astype(jnp.int16)


def encode(intensity, punch_radius):
    planes, h_block, k_block = intensity.shape
    hbm = pl.BlockSpec(memory_space=pltpu.HBM)
    across, down, nodes = h_block // SP + 1, k_block // SP + 1, punch_radius.shape[2]
    return pl.pallas_call(
        encode_kernel,
        in_specs=[hbm, hbm],
        out_specs=pl.BlockSpec(memory_space=pltpu.VMEM),
        out_shape=pltpu.VMEM((planes * CLASSES, 16, LANES), jnp.int16),
        scratch_shapes=[
            pltpu.VMEM((planes, k_block, h_block), F32),
            pltpu.VMEM((across, 2, nodes), jnp.int32),
            pltpu.VMEM((down, 2, nodes), jnp.int32),
            pltpu.VMEM((4, 128, LANES), F32),
            pltpu.VMEM((planes // 2, 128, LANES), jnp.int32),
            pltpu.VMEM((planes // 2, 128, LANES), jnp.int32),
            pltpu.SemaphoreType.DMA((6,)),
        ],
        compiler_params=pltpu.CompilerParams(vmem_limit_bytes=58 << 20),
    )(jnp.swapaxes(intensity, 1, 2), jnp.swapaxes(punch_radius, 0, 1))


def decoded(codes):
    u = codes.astype(jnp.int32).astype(F32) * (1.0 / CODE)
    return (u * u) * (u * jnp.abs(u))


def times(re, im, c, s):
    return re * c - im * s, re * s + im * c


def four(a, b, c, d):
    s_re, s_im = a[0] + c[0], a[1] + c[1]
    d_re, d_im = a[0] - c[0], a[1] - c[1]
    t_re, t_im = b[0] + d[0], b[1] + d[1]
    e_re, e_im = b[0] - d[0], b[1] - d[1]
    return (
        (s_re + t_re, s_im + t_im),
        (d_re - e_im, d_im + e_re),
        (s_re - t_re, s_im - t_im),
        (d_re + e_im, d_im - e_re),
    )


def eight(y):
    even = four(y[0], y[2], y[4], y[6])
    odd = four(y[1], y[3], y[5], y[7])
    root = float(np.sqrt(0.5))
    o1 = ((odd[1][0] - odd[1][1]) * root, (odd[1][0] + odd[1][1]) * root)
    o2 = (-odd[2][1], odd[2][0])
    o3 = (-(odd[3][0] + odd[3][1]) * root, (odd[3][0] - odd[3][1]) * root)
    odd = (odd[0], o1, o2, o3)
    first = [(e[0] + o[0], e[1] + o[1]) for e, o in zip(even, odd)]
    second = [(e[0] - o[0], e[1] - o[1]) for e, o in zip(even, odd)]
    return first + second


def column_kernel(codes_ref, order_ref, dft_ref, cos_ref, sin_ref, out_ref, s_ref, y_ref):
    sub = lax.broadcasted_iota(jnp.int32, (16, 8, LANES), 1)
    lane = lax.broadcasted_iota(jnp.int32, (8, 8, LANES), 2)
    for tile in range(N // LANES):
        row, upper = tile // 2, tile % 2
        got = decoded(codes_ref[32 * row : 32 * row + 32])[:, :8].reshape(16, 2, 8, LANES)
        even, odd = got[:, 0], got[:, 1]
        if upper:
            direct = jnp.where(sub < 4, pltpu.roll(even, 4, 1), odd)
        else:
            direct = jnp.where(sub < 4, even, pltpu.roll(odd, 4, 1))
        pair = [
            jnp.stack([decoded(codes_ref[32 * r + 2 * tile + j])[8:] for r in range(8)])
            for j in range(2)
        ]
        low = jnp.where(lane < 64, pair[0], pltpu.roll(pair[1], 64, 2))
        high = jnp.where(lane < 64, pltpu.roll(pair[0], 64, 2), pair[1])
        mirror = jnp.stack([low, high], axis=1)
        whole = (direct.reshape(128, LANES) + mirror.reshape(128, LANES)).astype(BF)
        turned = dot(order_ref[...], whole, (1, 1)).astype(BF)
        for a in range(8):
            lanes = slice(a * LANES, (a + 1) * LANES)
            s_ref[16 * tile : 16 * tile + 16, lanes] = turned[16 * a : 16 * a + 16]
    right = s_ref[...]
    right = jnp.concatenate([right, right], axis=0)
    for part in range(2):
        y_ref[256 * part : 256 * part + 256] = dot(dft_ref[256 * part : 256 * part + 256], right)
    for i in range(32):
        y = []
        for a in range(8):
            lanes = slice(a * LANES, (a + 1) * LANES)
            at = slice(8 * i, 8 * i + 8)
            here = 8 * i + i // 16 * 128
            re, im = y_ref[here : here + 8, lanes], y_ref[here + 128 : here + 136, lanes]
            if a:
                re, im = times(re, im, cos_ref[at, lanes], sin_ref[at, lanes])
            y.append((re, im))
        for c, (re, im) in enumerate(eight(y)):
            out_ref[32 * c + i] = jnp.concatenate([re, im], axis=0).astype(BF)


def column_tables():
    d = np.arange(256)
    cos, sin = wave(d[:, None] * d[None, :], 256)
    order = [cos[:128], sin[:128], cos[128:], sin[128:]]
    high, low = split_table(np.concatenate(order, axis=0))
    dft = np.concatenate([high, low], axis=1)
    cos, sin = wave(d[:, None] * np.repeat(np.arange(8), LANES)[None, :], N)
    order = np.zeros((LANES, LANES))
    order[np.arange(LANES), np.arange(LANES) % 16 * 8 + np.arange(LANES) // 16] = 1.0
    return order.astype(ml_dtypes.bfloat16), dft, cos.astype(np.float32), sin.astype(np.float32)


def columns(codes):
    vmem = pl.BlockSpec(memory_space=pltpu.VMEM)
    return pl.pallas_call(
        column_kernel,
        in_specs=[vmem] * 5,
        out_specs=vmem,
        out_shape=jax.ShapeDtypeStruct((256, 16, LANES), BF),
        scratch_shapes=[pltpu.VMEM((256, 8 * LANES), BF), pltpu.VMEM((512, 8 * LANES), F32)],
        compiler_params=pltpu.CompilerParams(vmem_limit_bytes=40 << 20),
    )(codes, *map(jnp.asarray, column_tables()))


def sixteen(y):
    first = [four(y[i], y[i + 4], y[i + 8], y[i + 12]) for i in range(4)]
    out = [None] * 16
    for k in range(4):
        turned = []
        for i in range(4):
            re, im = first[i][k]
            if i * k:
                angle = 2.0 * np.pi * i * k / 16
                c, s = float(np.cos(angle)), float(np.sin(angle))
                if i * k == 4:
                    re, im = -im, re
                elif i * k == 2:
                    re, im = (re - im) * c, (re + im) * c
                elif i * k == 6:
                    re, im = -(re + im) * s, (re - im) * s
                else:
                    re, im = times(re, im, c, s)
            turned.append((re, im))
        for j, value in enumerate(four(*turned)):
            out[k + 4 * j] = value
    return out


def row_kernel(x_ref, dft_ref, cos_ref, sin_ref, re_hbm, im_hbm, re_ref, im_ref, y_ref, sems):
    copies = []

    def matmul(i):
        x = x_ref[CLASSES * i : CLASSES * (i + 1)].astype(F32)
        real = x[:, :8].reshape(CLASSES * 8, LANES).astype(BF)
        imag = x[:, 8:].reshape(CLASSES * 8, LANES).astype(BF)
        y_ref[i] = dot(jnp.concatenate([real, imag, real, imag], axis=1), dft_ref[...])

    matmul(0)
    for i in range(PLANES):
        if i + 1 < PLANES:
            matmul(i + 1)
        y = []
        for m in range(CLASSES):
            re, im = y_ref[i, 8 * m : 8 * m + 8, :LANES], y_ref[i, 8 * m : 8 * m + 8, LANES:]
            if m:
                re, im = times(re, im, cos_ref[m : m + 1], sin_ref[m : m + 1])
            y.append((re, im))
        for d, (re, im) in enumerate(sixteen(y)):
            re_ref[i, :, d * LANES : (d + 1) * LANES] = re
            im_ref[i, :, d * LANES : (d + 1) * LANES] = im
        if i % 2:
            done = pl.ds(i - 1, 2)
            pairs = ((re_ref, re_hbm), (im_ref, im_hbm))
            for which, (here, there) in enumerate(pairs):
                copy = pltpu.make_async_copy(here.at[done], there.at[done], sems.at[i // 2, which])
                copy.start()
                copies.append(copy)
    for copy in copies:
        copy.wait()


def row_tables():
    t = np.arange(LANES)
    cos, sin = wave(t[:, None] * t[None, :], LANES)
    both = [np.concatenate([cos, sin], axis=1), np.concatenate([-sin, cos], axis=1)]
    high, low = split_table(np.concatenate(both, axis=0) / N)
    cos, sin = wave(np.arange(CLASSES)[:, None] * t[None, :], N)
    return np.concatenate([high, low], axis=0), cos.astype(np.float32), sin.astype(np.float32)


def rows(spectra):
    vmem, hbm = pl.BlockSpec(memory_space=pltpu.VMEM), pl.BlockSpec(memory_space=pltpu.HBM)
    shape = jax.ShapeDtypeStruct((PLANES, 8, N), F32)
    return pl.pallas_call(
        row_kernel,
        in_specs=[vmem] * 4,
        out_specs=[hbm, hbm],
        out_shape=[shape, shape],
        scratch_shapes=[
            pltpu.VMEM((PLANES, 8, N), F32),
            pltpu.VMEM((PLANES, 8, N), F32),
            pltpu.VMEM((PLANES, 128, 256), F32),
            pltpu.SemaphoreType.DMA((PLANES // 2, 2)),
        ],
        compiler_params=pltpu.CompilerParams(vmem_limit_bytes=40 << 20),
    )(spectra, *map(jnp.asarray, row_tables()))


def exchange(array):
    return lax.all_to_all(array, ("row", "col"), split_axis=0, concat_axis=0, tiled=True)


def body(intensity, punch_radius):
    codes = exchange(encode(intensity, punch_radius))
    spectra = exchange(columns(codes))
    return tuple(rows(spectra))


def solution(mesh):
    in_specs = (P(None, "row", "col"), P())
    out_specs = (P(None, ("row", "col"), None), P(None, ("row", "col"), None))
    return jax.shard_map(body, mesh=mesh, in_specs=in_specs, out_specs=out_specs, check_vma=False)
```

```python
import jax
import jax.numpy as jnp
import ml_dtypes
import numpy as np
from jax import lax
from jax.experimental import pallas as pl
from jax.experimental.pallas import tpu as pltpu
from jax.sharding import PartitionSpec as P

N = 2048
SP = 16
PLANES = 16
CLASSES = 16
OWN = N // CLASSES
LANES = 128
CODE = 2.0**14.25
BF = jnp.bfloat16
F32 = jnp.float32


def dot(left, right, contract=(1, 0)):
    dims = (((contract[0],), (contract[1],)), ((), ()))
    return lax.dot_general(left, right, dims, preferred_element_type=F32)


def split_table(table):
    high = table.astype(ml_dtypes.bfloat16)
    low = (table - high.astype(np.float64)).astype(ml_dtypes.bfloat16)
    return high, low


def wave(phases, period):
    angles = 2.0 * np.pi * (phases % period) / period
    return np.cos(angles), np.sin(angles)


def encode_kernel(x_hbm, table_hbm, code_ref, x_ref, near_h, near_k, g_ref, e_ref, t_ref, sems):
    half = LANES // 2
    row_at, col_at = lax.axis_index("row"), lax.axis_index("col")
    across, down = near_h.shape[0], near_k.shape[0]
    tables = [
        pltpu.make_async_copy(table_hbm.at[pl.ds(16 * row_at, across)], near_h, sems.at[4]),
        pltpu.make_async_copy(table_hbm.at[pl.ds(4 * col_at, down)], near_k, sems.at[5]),
    ]
    chunks = [
        pltpu.make_async_copy(x_hbm.at[pl.ds(4 * j, 4)], x_ref.at[pl.ds(4 * j, 4)], sems.at[j])
        for j in range(4)
    ]
    for copy in tables + chunks:
        copy.start()

    def picks(shape, base):
        places = lax.broadcasted_iota(jnp.int32, shape, 0)
        nodes = lax.broadcasted_iota(jnp.int32, shape, 1)
        return ((base + places + SP // 2) // SP == nodes).astype(F32).astype(BF)

    h_any, k_any = picks((256, table_hbm.shape[2]), 256 * row_at), picks((64, table_hbm.shape[2]), 64 * col_at)
    h_own, k_own = picks((256, across), 0), picks((64, down), 0)
    off_h = (lax.broadcasted_iota(jnp.int32, (64, 256), 1) + SP // 2) % SP - SP // 2
    off_k = (lax.broadcasted_iota(jnp.int32, (64, 256), 0) + SP // 2) % SP - SP // 2
    near = (off_h * off_h + off_k * off_k).astype(F32)
    for copy in tables:
        copy.wait()
    for s in range(2):
        keep = dot(k_any, near_h[:, s, :].astype(F32).astype(BF), (1, 1)).astype(BF)
        keep = dot(keep, h_own, (1, 1)) - near
        swap = dot(k_own, near_k[:, s, :].astype(F32).astype(BF)).astype(BF)
        swap = dot(swap, h_any, (1, 1)) - near
        for side, g in enumerate((keep, swap)):
            g_ref[2 * s + side] = jnp.concatenate([g[:, :128], g[:, 128:]], axis=0)

    def coded(level):
        node = (level + SP // 2) // SP
        far = float((level - SP * node) ** 2)
        x = x_ref[level]
        packed = jnp.concatenate([x[:, :128], x[:, 128:]], axis=0)
        keep = far >= g_ref[2 * node]
        swap = far >= g_ref[2 * node + 1]
        value = jnp.where(keep, packed * jnp.where(swap, 0.5, 1.0), 0.0)
        size = lax.rsqrt(lax.rsqrt(jnp.abs(value))) * CODE + 0.5
        size = size.astype(jnp.int32)
        return jnp.where(value < 0.0, -size, size)

    for pair in range(PLANES // 2):
        if pair % 2 == 0:
            chunks[pair // 2].wait()
        word = (coded(2 * pair) << 16) | (coded(2 * pair + 1) & 0xFFFF)
        t_ref[pair] = word
        e_ref[pair] = word.T
        for m in range(CLASSES):
            direct = t_ref[pair, pl.ds(m, 8, stride=CLASSES), :]
            mirror = e_ref[pair, pl.ds(m, 8, stride=CLASSES), :]
            both = jnp.concatenate([direct, mirror], axis=0)
            code_ref[2 * pair * CLASSES + m] = (both >> 16).astype(jnp.int16)
            code_ref[(2 * pair + 1) * CLASSES + m] = ((both << 16) >> 16).astype(jnp.int16)


def encode(intensity, punch_radius):
    planes, h_block, k_block = intensity.shape
    hbm = pl.BlockSpec(memory_space=pltpu.HBM)
    across, down, nodes = h_block // SP + 1, k_block // SP + 1, punch_radius.shape[2]
    return pl.pallas_call(
        encode_kernel,
        in_specs=[hbm, hbm],
        out_specs=pl.BlockSpec(memory_space=pltpu.VMEM),
        out_shape=pltpu.VMEM((planes * CLASSES, 16, LANES), jnp.int16),
        scratch_shapes=[
            pltpu.VMEM((planes, k_block, h_block), F32),
            pltpu.VMEM((across, 2, nodes), jnp.int32),
            pltpu.VMEM((down, 2, nodes), jnp.int32),
            pltpu.VMEM((4, 128, LANES), F32),
            pltpu.VMEM((planes // 2, 128, LANES), jnp.int32),
            pltpu.VMEM((planes // 2, 128, LANES), jnp.int32),
            pltpu.SemaphoreType.DMA((6,)),
        ],
        compiler_params=pltpu.CompilerParams(vmem_limit_bytes=58 << 20),
    )(jnp.swapaxes(intensity, 1, 2), jnp.swapaxes(punch_radius, 0, 1))


def decoded(codes):
    u = codes.astype(jnp.int32).astype(F32)
    return (u * u) * (u * jnp.abs(u))


def times(re, im, c, s):
    return re * c - im * s, re * s + im * c


def four(a, b, c, d):
    s_re, s_im = a[0] + c[0], a[1] + c[1]
    d_re, d_im = a[0] - c[0], a[1] - c[1]
    t_re, t_im = b[0] + d[0], b[1] + d[1]
    e_re, e_im = b[0] - d[0], b[1] - d[1]
    return (
        (s_re + t_re, s_im + t_im),
        (d_re - e_im, d_im + e_re),
        (s_re - t_re, s_im - t_im),
        (d_re + e_im, d_im - e_re),
    )


def eight(y):
    even = four(y[0], y[2], y[4], y[6])
    odd = four(y[1], y[3], y[5], y[7])
    root = float(np.sqrt(0.5))
    o1 = ((odd[1][0] - odd[1][1]) * root, (odd[1][0] + odd[1][1]) * root)
    o2 = (-odd[2][1], odd[2][0])
    o3 = (-(odd[3][0] + odd[3][1]) * root, (odd[3][0] - odd[3][1]) * root)
    odd = (odd[0], o1, o2, o3)
    first = [(e[0] + o[0], e[1] + o[1]) for e, o in zip(even, odd)]
    second = [(e[0] - o[0], e[1] - o[1]) for e, o in zip(even, odd)]
    return first + second


def column_kernel(codes_ref, order_ref, dft_ref, cos_ref, sin_ref, out_ref, s_ref, y_ref):
    sub = lax.broadcasted_iota(jnp.int32, (16, 8, LANES), 1)
    lane = lax.broadcasted_iota(jnp.int32, (8, 8, LANES), 2)
    for tile in range(N // LANES):
        row, upper = tile // 2, tile % 2
        got = decoded(codes_ref[32 * row : 32 * row + 32])[:, :8].reshape(16, 2, 8, LANES)
        even, odd = got[:, 0], got[:, 1]
        if upper:
            direct = jnp.where(sub < 4, pltpu.roll(even, 4, 1), odd)
        else:
            direct = jnp.where(sub < 4, even, pltpu.roll(odd, 4, 1))
        pair = [
            jnp.stack([decoded(codes_ref[32 * r + 2 * tile + j])[8:] for r in range(8)])
            for j in range(2)
        ]
        low = jnp.where(lane < 64, pair[0], pltpu.roll(pair[1], 64, 2))
        high = jnp.where(lane < 64, pltpu.roll(pair[0], 64, 2), pair[1])
        mirror = jnp.stack([low, high], axis=1)
        whole = (direct.reshape(128, LANES) + mirror.reshape(128, LANES)).astype(BF)
        turned = dot(order_ref[...], whole, (1, 1)).astype(BF)
        for a in range(8):
            lanes = slice(a * LANES, (a + 1) * LANES)
            s_ref[16 * tile : 16 * tile + 16, lanes] = turned[16 * a : 16 * a + 16]
    right = s_ref[...]
    right = jnp.concatenate([right, right], axis=0)
    for part in range(2):
        y_ref[256 * part : 256 * part + 256] = dot(dft_ref[256 * part : 256 * part + 256], right)
    for i in range(32):
        y = []
        for a in range(8):
            lanes = slice(a * LANES, (a + 1) * LANES)
            at = slice(8 * i, 8 * i + 8)
            here = 8 * i + i // 16 * 128
            re, im = y_ref[here : here + 8, lanes], y_ref[here + 128 : here + 136, lanes]
            if a:
                re, im = times(re, im, cos_ref[at, lanes], sin_ref[at, lanes])
            y.append((re, im))
        for c, (re, im) in enumerate(eight(y)):
            out_ref[32 * c + i] = jnp.concatenate([re, im], axis=0).astype(BF)


def column_tables():
    d = np.arange(256)
    cos, sin = wave(d[:, None] * d[None, :], 256)
    order = [cos[:128], sin[:128], cos[128:], sin[128:]]
    high, low = split_table(np.concatenate(order, axis=0) * 2.0**-57)
    dft = np.concatenate([high, low], axis=1)
    cos, sin = wave(d[:, None] * np.repeat(np.arange(8), LANES)[None, :], N)
    order = np.zeros((LANES, LANES))
    order[np.arange(LANES), np.arange(LANES) % 16 * 8 + np.arange(LANES) // 16] = 1.0
    return order.astype(ml_dtypes.bfloat16), dft, cos.astype(np.float32), sin.astype(np.float32)


def columns(codes):
    vmem = pl.BlockSpec(memory_space=pltpu.VMEM)
    return pl.pallas_call(
        column_kernel,
        in_specs=[vmem] * 5,
        out_specs=vmem,
        out_shape=jax.ShapeDtypeStruct((256, 16, LANES), BF),
        scratch_shapes=[pltpu.VMEM((256, 8 * LANES), BF), pltpu.VMEM((512, 8 * LANES), F32)],
        compiler_params=pltpu.CompilerParams(vmem_limit_bytes=40 << 20),
    )(codes, *map(jnp.asarray, column_tables()))


def sixteen(y):
    first = [four(y[i], y[i + 4], y[i + 8], y[i + 12]) for i in range(4)]
    out = [None] * 16
    for k in range(4):
        turned = []
        for i in range(4):
            re, im = first[i][k]
            if i * k:
                angle = 2.0 * np.pi * i * k / 16
                c, s = float(np.cos(angle)), float(np.sin(angle))
                if i * k == 4:
                    re, im = -im, re
                elif i * k == 2:
                    re, im = (re - im) * c, (re + im) * c
                elif i * k == 6:
                    re, im = -(re + im) * s, (re - im) * s
                else:
                    re, im = times(re, im, c, s)
            turned.append((re, im))
        for j, value in enumerate(four(*turned)):
            out[k + 4 * j] = value
    return out


def row_kernel(x_ref, dft_ref, cos_ref, sin_ref, re_hbm, im_hbm, re_ref, im_ref, y_ref, sems):
    copies = []

    def matmul(i):
        x = x_ref[CLASSES * i : CLASSES * (i + 1)].astype(F32)
        real = x[:, :8].reshape(CLASSES * 8, LANES).astype(BF)
        imag = x[:, 8:].reshape(CLASSES * 8, LANES).astype(BF)
        y_ref[i] = dot(jnp.concatenate([real, imag, real, imag], axis=1), dft_ref[...])

    matmul(0)
    for i in range(PLANES):
        if i + 1 < PLANES:
            matmul(i + 1)
        y = []
        for m in range(CLASSES):
            re, im = y_ref[i, 8 * m : 8 * m + 8, :LANES], y_ref[i, 8 * m : 8 * m + 8, LANES:]
            if m:
                re, im = times(re, im, cos_ref[m : m + 1], sin_ref[m : m + 1])
            y.append((re, im))
        for d, (re, im) in enumerate(sixteen(y)):
            re_ref[i, :, d * LANES : (d + 1) * LANES] = re
            im_ref[i, :, d * LANES : (d + 1) * LANES] = im
        if i % 2:
            done = pl.ds(i - 1, 2)
            pairs = ((re_ref, re_hbm), (im_ref, im_hbm))
            for which, (here, there) in enumerate(pairs):
                copy = pltpu.make_async_copy(here.at[done], there.at[done], sems.at[i // 2, which])
                copy.start()
                copies.append(copy)
    for copy in copies:
        copy.wait()


def row_tables():
    t = np.arange(LANES)
    cos, sin = wave(t[:, None] * t[None, :], LANES)
    both = [np.concatenate([cos, sin], axis=1), np.concatenate([-sin, cos], axis=1)]
    high, low = split_table(np.concatenate(both, axis=0) / N)
    cos, sin = wave(np.arange(CLASSES)[:, None] * t[None, :], N)
    return np.concatenate([high, low], axis=0), cos.astype(np.float32), sin.astype(np.float32)


def rows(spectra):
    vmem, hbm = pl.BlockSpec(memory_space=pltpu.VMEM), pl.BlockSpec(memory_space=pltpu.HBM)
    shape = jax.ShapeDtypeStruct((PLANES, 8, N), F32)
    return pl.pallas_call(
        row_kernel,
        in_specs=[vmem] * 4,
        out_specs=[hbm, hbm],
        out_shape=[shape, shape],
        scratch_shapes=[
            pltpu.VMEM((PLANES, 8, N), F32),
            pltpu.VMEM((PLANES, 8, N), F32),
            pltpu.VMEM((PLANES, 128, 256), F32),
            pltpu.SemaphoreType.DMA((PLANES // 2, 2)),
        ],
        compiler_params=pltpu.CompilerParams(vmem_limit_bytes=40 << 20),
    )(spectra, *map(jnp.asarray, row_tables()))


def exchange(array):
    return lax.all_to_all(array, ("row", "col"), split_axis=0, concat_axis=0, tiled=True)


def body(intensity, punch_radius):
    codes = exchange(encode(intensity, punch_radius))
    spectra = exchange(columns(codes))
    return tuple(rows(spectra))


def solution(mesh):
    in_specs = (P(None, "row", "col"), P())
    out_specs = (P(None, ("row", "col"), None), P(None, ("row", "col"), None))
    return jax.shard_map(body, mesh=mesh, in_specs=in_specs, out_specs=out_specs, check_vma=False)
```
